128 devices in a mesh: rows: 16 (over z, x_lo, core), ch: 8 (over x_hi, y).
Axes of the slice: x: 4 (x_hi: 2, x_lo: 2; x = x_hi * 2 + x_lo), y: 4, z: 4, core: 2. Of those that a mesh axis runs over, the one named last changes fastest.
Arguments:
- x_band: bfloat16 [512, 128, 128], P('ch', 'rows'), may hold values from -40 to 40
- first_filter: bfloat16 [3, 3, 512, 512], P(None, None, 'ch'), may hold values from -0.09375 to 0.09375
- second_filter: bfloat16 [3, 3, 512, 512], P(None, None, 'ch'), may hold values from -0.09375 to 0.09375
- norm_gain: float32 [512], P('ch'), may hold values from 0.5 to 2
- norm_shift: float32 [512], P('ch'), may hold values from -3 to 3
- out_cotangent: bfloat16 [512, 128, 128], P('ch', 'rows'), may hold values from -6 to 6
Outputs:
- band_grad: bfloat16 [512, 128, 128], P('ch', 'rows')
- first_grad: float32 [3, 3, 512, 512], P(None, None, 'ch')
- second_grad: float32 [3, 3, 512, 512], P(None, None, 'ch')
- gain_grad: float32 [512], P('ch')
- shift_grad: float32 [512], P('ch')
The draws below stay inside these ranges and needn't reach their ends.
All inputs are finite; a program needn't handle non-finite values.
Results may differ from the reference program's by a relative error of at most 0.028.
Values may be sent and summed in bfloat16 or wider, within the bound.
No kernel may reach another device: no remote copies, remote signals or barrier semaphores. Data moves between devices by JAX's collectives and lax.ppermute only.
A program may use at most 128 MiB of HBM per device.

```python
import math
import jax
import jax.numpy as jnp
from jax import lax

C = 512
G = 32
W = 128
HEIGHT = 128
N_CH = 8


def draw_x_band(key, part):
    key = jax.random.fold_in(key, 5)
    noise_key = jax.random.fold_in(key, 0)
    row_place = jnp.arange(HEIGHT, dtype=jnp.float32) / (HEIGHT - 1.0)
    noise = jnp.clip(jax.random.normal(noise_key, (C, HEIGHT, W), jnp.float32), -4.0, 4.0)
    rising = jnp.exp(math.log(3.0) * row_place)[None, :, None]
    values = noise * rising
    return values.astype(jnp.bfloat16)


def block_scale(rng, shape, cuts, low, high):
    gain, own = 1.0, jax.random.fold_in(rng, 6)
    for position, blocks in cuts:
        heights = jnp.exp(jax.random.uniform(jax.random.fold_in(own, position), (blocks,), jnp.float32, low / len(cuts), high / len(cuts)))
        gain = gain * jnp.repeat(heights, shape[position] // blocks).reshape([-1 if axis == position else 1 for axis in range(len(shape))])
    return gain


def centred(own_key, dims, width, reach, pieces=(), held_as=jnp.bfloat16):
    loudness = block_scale(own_key, dims, pieces, -0.22, 0.18) if pieces else 1.0
    values = jax.random.normal(own_key, dims, jnp.float32) * width * loudness
    return jnp.minimum(jnp.maximum(values, -reach), reach).astype(held_as)


def setup_inputs(seed: int = 0) -> dict:
    keys = jax.random.split(jax.random.key(seed), 7)
    return {
        "x_band": draw_x_band(jax.random.fold_in(keys[6], 71), 0),
        "first_filter": centred(keys[1], (3, 3, C, C), (9 * C) ** -0.5, 0.09375, ((2, 8),)),
        "second_filter": centred(keys[2], (3, 3, C, C), (9 * C) ** -0.5, 0.09375, ((2, 8),)),
        "norm_gain": jnp.clip(0.5 + 1.5 * jax.random.uniform(keys[3], (C,), jnp.float32) ** block_scale(keys[3], (C,), ((0, 8),), -0.2, 0.2), 0.5, 2.0),
        "norm_shift": centred(keys[4], (C,), 0.5, 3.0, ((0, 8),), jnp.float32),
        "out_cotangent": centred(keys[5], (C, HEIGHT, W), 1.0, 6.0, ((0, 8), (1, 16))),
    }


epsilon = 1e-06

def pad_band(values):
    return jnp.pad(values, ((0, 0), (1, 1), (1, 1)))

def conv_taps(padded, weight, height, breadth):
    running = jnp.zeros((weight.shape[2], height * breadth), jnp.float32)
    for row_tap in range(3):
        for col_tap in range(3):
            slab = padded[:, row_tap:row_tap + height, col_tap:col_tap + breadth].reshape(padded.shape[0], -1)
            running = running + jnp.dot(weight[row_tap, col_tap], slab, preferred_element_type=jnp.float32)
    return running

def filter_taps(gradient, padded, height, breadth):
    outer = []
    for row_tap in range(3):
        inner = []
        for col_tap in range(3):
            slab = padded[:, row_tap:row_tap + height, col_tap:col_tap + breadth].reshape(padded.shape[0], -1)
            inner.append(lax.dot_general(gradient, slab, (((1,), (1,)), ((), ())), preferred_element_type=jnp.float32))
        outer.append(jnp.stack(inner))
    return jnp.stack(outer)

def transpose_taps(weight, padded, height, breadth):
    running = jnp.zeros((weight.shape[3], height * breadth), jnp.float32)
    for row_tap in range(3):
        for col_tap in range(3):
            slab = padded[:, 2 - row_tap:2 - row_tap + height, 2 - col_tap:2 - col_tap + breadth].reshape(padded.shape[0], -1)
            running = running + lax.dot_general(weight[row_tap, col_tap], slab, (((0,), (0,)), ((), ())), preferred_element_type=jnp.float32)
    return running

def blocked_input(gradient, weight, height, breadth):
    padded = pad_band(gradient)
    block_width = C // N_CH
    running = jnp.zeros((C, height * breadth), jnp.float32)
    for block in range(N_CH):
        lower = block * block_width
        partial_sum = transpose_taps(weight[:, :, lower:lower + block_width, :], padded[lower:lower + block_width], height, breadth)
        running = running + lax.optimization_barrier(partial_sum.astype(jnp.bfloat16)).astype(jnp.float32)
    return running

def reference(x_band, first_filter, second_filter, norm_gain, norm_shift, out_cotangent):
    chans, height, breadth = x_band.shape
    group_size = C // G
    x_pad = pad_band(x_band)
    hidden = conv_taps(x_pad, first_filter, height, breadth)
    grouped = hidden.reshape(G, -1)
    cell_count = group_size * height * breadth
    group_mean = lax.optimization_barrier(jnp.sum(grouped, axis=1)) / cell_count
    group_var = lax.optimization_barrier(jnp.sum(grouped * grouped, axis=1)) / cell_count - group_mean * group_mean
    inv_std = lax.rsqrt(group_var + epsilon)
    channel_mean = jnp.repeat(group_mean, group_size)
    channel_scale = jnp.repeat(inv_std, group_size)
    normed = (hidden - channel_mean[:, None]) * channel_scale[:, None]
    shifted = normed * norm_gain[:, None] + norm_shift[:, None]
    squashed = jax.nn.sigmoid(shifted)
    activation = (shifted * squashed).astype(jnp.bfloat16).reshape(chans, height, breadth)
    act_pad = pad_band(activation)
    second_grad = filter_taps(out_cotangent.reshape(chans, -1), act_pad, height, breadth)
    act_grad = blocked_input(out_cotangent, second_filter, height, breadth)
    pre_grad = act_grad * squashed * (1.0 + shifted * (1.0 - squashed))
    gain_grad = lax.optimization_barrier(jnp.sum(pre_grad * normed, axis=1))
    shift_grad = lax.optimization_barrier(jnp.sum(pre_grad, axis=1))
    first_term = lax.optimization_barrier(jnp.sum((norm_gain * shift_grad).reshape(G, group_size), axis=1)) / cell_count
    second_term = lax.optimization_barrier(jnp.sum((norm_gain * gain_grad).reshape(G, group_size), axis=1)) / cell_count
    hidden_grad = channel_scale[:, None] * (pre_grad * norm_gain[:, None] - jnp.repeat(first_term, group_size)[:, None] - normed * jnp.repeat(second_term, group_size)[:, None])
    hidden_grad = hidden_grad.astype(jnp.bfloat16)
    first_grad = filter_taps(hidden_grad, x_pad, height, breadth)
    band_grad = blocked_input(hidden_grad.reshape(chans, height, breadth), first_filter, height, breadth)
    band_grad = band_grad.reshape(chans, height, breadth).astype(jnp.bfloat16)
    return (band_grad, first_grad, second_grad, gain_grad, shift_grad)
```

```python
import functools

import jax
import jax.numpy as jnp
from jax import lax
from jax.experimental import pallas as pl
from jax.experimental.pallas import tpu as pltpu
from jax.sharding import PartitionSpec as P

C = 512
G = 32
EPS = 1e-06
ROWS = 8
W = 128
OWN = 64
TAPS = 9
STACK = TAPS * OWN
PIECE = 144
BF = jnp.bfloat16
F32 = jnp.float32

VMEM = pl.BlockSpec(memory_space=pltpu.VMEM)
SMEM = pl.BlockSpec(memory_space=pltpu.SMEM)

CH_SHIFTS = ((0, 0), (1, 0), (0, 1), (0, 3), (0, 2), (1, 1), (1, 3), (1, 2))


def ch_pairs(dx, dy):
    return [(i, ((i // 4 + dx) % 2) * 4 + (i % 4 + dy) % 4) for i in range(8)]


def row_pairs(dz, dx, dc):
    pairs = []
    for i in range(16):
        z, x, c = i // 4, (i // 2) % 2, i % 2
        pairs.append((i, ((z + dz) % 4) * 4 + ((x + dx) % 2) * 2 + (c + dc) % 2))
    return pairs


def call(kernel, out, *args, flops=0, name=None):
    moved = sum(a.size * a.dtype.itemsize for a in args)
    shapes = [jax.ShapeDtypeStruct(s, d) for s, d in out["shapes"]]
    moved += sum(s.size * s.dtype.itemsize for s in shapes)
    return pl.pallas_call(
        kernel,
        out_shape=shapes,
        in_specs=[SMEM if a.dtype == jnp.int32 else VMEM for a in args],
        out_specs=[VMEM] * len(shapes),
        scratch_shapes=out.get("scratch", ()),
        compiler_params=pltpu.CompilerParams(vmem_limit_bytes=40 * 1024 * 1024),
        cost_estimate=pl.CostEstimate(flops=flops, bytes_accessed=moved, transcendentals=0),
        name=name,
    )(*args)


def shifted_cols(v, by):
    lane = lax.broadcasted_iota(jnp.int32, v.shape, 1)
    rolled = pltpu.roll(v, by % W, 1)
    return jnp.where(lane == (0 if by == 1 else W - 1), 0.0, rolled)


def source_of(at, shift):
    dx, dy = shift
    return lax.rem(at[0] + dx, 2) * 4 + lax.rem(at[1] + 4 - dy, 4)


def target_of(at, shift):
    dx, dy = shift
    return lax.rem(at[0] + dx, 2) * 4 + lax.rem(at[1] + dy, 4)


def assemble(at, pieces, full):
    for shift, piece in zip(CH_SHIFTS, pieces):
        place = pl.multiple_of(source_of(at, shift) * OWN, OWN)
        full[:, pl.ds(place, OWN), :] = piece[...]


def conv_kernel(at, *refs):
    pieces, (w, hid, top, bottom, full, acc) = refs[:8], refs[8:]
    assemble(at, pieces, full)
    acc[...] = jnp.zeros_like(acc)
    for j in range(ROWS // 2):
        pair = jnp.concatenate([full[2 * j], full[2 * j + 1]], axis=1)
        v = jnp.dot(w[...], pair, preferred_element_type=F32)
        for a in range(3):
            for b in range(3):
                for k in range(2):
                    o = (a * 3 + b) * OWN
                    acc[b, 2 * j + k - a + 2] += v[o : o + OWN, k * W : (k + 1) * W]
    for r in range(ROWS + 2):
        row = acc[1, r] + shifted_cols(acc[0, r], 1) + shifted_cols(acc[2, r], -1)
        if r == 0:
            top[...] = row
        elif r == ROWS + 1:
            bottom[...] = row
        else:
            hid[r - 1] = row


def stats_kernel(hid, above, below, out, stats):
    total = jnp.zeros((OWN, W), F32)
    square = jnp.zeros((OWN, W), F32)
    for r in range(ROWS):
        row = hid[r]
        if r == 0:
            row = row + above[...]
        if r == ROWS - 1:
            row = row + below[...]
        out[r] = row
        total = total + row
        square = square + row * row
    both = jnp.concatenate([total, square], axis=0)
    sums = jnp.sum(jnp.sum(both.reshape(8, OWN // 4, W), axis=1), axis=1, keepdims=True)
    stats[...] = jnp.broadcast_to(sums, (8, W))


def per_channel(groups):
    return jnp.broadcast_to(groups[:, None, :], (4, OWN // 4, W)).reshape(OWN, W)


def norm_of(stats, cells):
    mean = stats[0:4] / cells
    var = stats[4:8] / cells - mean * mean
    return per_channel(mean), per_channel(lax.rsqrt(var + EPS))


def act_kernel(cells, hid, stats, gain, shift, act):
    mean, scale = norm_of(stats[...], cells)
    for r in range(ROWS):
        normed = (hid[r] - mean) * scale
        s = normed * gain[...] + shift[...]
        act[r] = (s * jax.nn.sigmoid(s)).astype(BF)


def pre_kernel(cells, hid, stats, gain, shift, p0, p1, p2, p3, p4, pre, sums):
    mean, scale = norm_of(stats[...], cells)
    by_normed = jnp.zeros((OWN, W), F32)
    plain = jnp.zeros((OWN, W), F32)
    for r in range(ROWS):
        normed = (hid[r] - mean) * scale
        s = normed * gain[...] + shift[...]
        q = jax.nn.sigmoid(s)
        act_grad = p0[r].astype(F32)
        for p in (p1, p2, p3, p4):
            act_grad = act_grad + p[r].astype(F32)
        value = act_grad * q * (1.0 + s * (1.0 - q))
        pre[r] = value
        by_normed = by_normed + value * normed
        plain = plain + value
    both = jnp.concatenate([by_normed, plain], axis=0).T
    sums[...] = jnp.broadcast_to(jnp.sum(both, axis=0, keepdims=True), (8, W))


def hidden_grad_kernel(cells, hid, stats, gain, pre, sums, out):
    mean, scale = norm_of(stats[...], cells)
    spread = jnp.broadcast_to(sums[0:1, :], (W, W)).T
    by_normed, plain = spread[:OWN], spread[OWN:]

    def group_mean(v):
        return per_channel(jnp.sum((gain[...] * v).reshape(4, OWN // 4, W), axis=1) / cells)

    first, second = group_mean(plain), group_mean(by_normed)
    for r in range(ROWS):
        normed = (hid[r] - mean) * scale
        out[r] = (scale * (pre[r] * gain[...] - first - normed * second)).astype(BF)


def input_grad_kernel(at, grad, above, below, wt, stack, *rest):
    pieces, (cols, full) = rest[:8], rest[8:]
    for r in range(ROWS + 2):
        row = above[...] if r == 0 else below[...] if r == ROWS + 1 else grad[r - 1]
        wide = row.astype(F32)
        cols[0, r] = shifted_cols(wide, -1).astype(BF)
        cols[1, r] = row
        cols[2, r] = shifted_cols(wide, 1).astype(BF)
    for j in range(ROWS // 2):
        for a in range(3):
            for b in range(3):
                o = (a * 3 + b) * OWN
                for k in range(2):
                    y = 2 * j + k
                    stack[o : o + OWN, y * W : (y + 1) * W] = cols[b, y - a + 2]
        part = jnp.dot(
            wt[...], stack[:, 2 * j * W : (2 * j + 2) * W], preferred_element_type=F32
        ).astype(BF)
        full[2 * j] = part[:, :W]
        full[2 * j + 1] = part[:, W:]
    for shift, piece in zip(CH_SHIFTS, pieces):
        place = pl.multiple_of(target_of(at, shift) * OWN, OWN)
        piece[...] = full[:, pl.ds(place, OWN), :]


def filter_products(at, stack, full, keep, send):
    core = at[4]
    for q in range(4):
        cells = jnp.concatenate(
            [full[r, q * W : (q + 1) * W, :] for r in range(ROWS)], axis=1
        )
        part = lax.dot_general(
            stack[...], cells, (((1,), (1,)), ((), ())), preferred_element_type=F32
        ).astype(BF)
        mine = core == q // 2

        @pl.when(mine)
        def _():
            keep[(q % 2) * STACK : (q % 2 + 1) * STACK, :] = part

        @pl.when(jnp.logical_not(mine))
        def _():
            send[(q % 2) * STACK : (q % 2 + 1) * STACK, :] = part


def filter_kernel(at, stack, full, keep, send):
    filter_products(at, stack, full, keep, send)


def gathered_filter_kernel(at, stack, *refs):
    pieces, (keep, send, full) = refs[:8], refs[8:]
    assemble(at, pieces, full)
    filter_products(at, stack, full, keep, send)


def core_sum_kernel(at, k1, r1, k2, r2, near, far):
    for n, (k, r) in enumerate(((k1, r1), (k2, r2))):
        for dx, out in ((0, near), (1, far)):
            for dz in range(4):
                p = lax.rem(at[3] + dx, 2) * 4 + lax.rem(at[2] + dz, 4)
                at_row = pl.ds(pl.multiple_of(p * PIECE, PIECE), PIECE)
                out[dz, n] = (k[at_row, :].astype(F32) + r[at_row, :].astype(F32)).astype(BF)


def pair_sum_kernel(near, far, z0, z1, z2, z3):
    for dz, out in enumerate((z0, z1, z2, z3)):
        out[...] = (near[dz].astype(F32) + far[dz].astype(F32)).astype(BF)


def four_sum_kernel(a, b, c, d, out):
    total = a[...].astype(F32) + b[...].astype(F32) + c[...].astype(F32) + d[...].astype(F32)
    out[...] = total.astype(BF)


def sum_four(a, b, c, d, name):
    return call(four_sum_kernel, dict(shapes=[(a.shape, BF)]), a, b, c, d, name=name)[0]


def place_kernel(at, mine, other, first, second):
    for half, src in ((0, mine), (1, other)):
        core = lax.rem(at[4] + half, 2)
        for k, (dz, dx) in enumerate(AG_ORDER):
            z, x = lax.rem(at[2] + 4 - dz, 4), lax.rem(at[3] + dx, 2)
            rows = pl.ds(pl.multiple_of(z * PIECE, PIECE), PIECE)
            lanes = pl.ds(pl.multiple_of((core * 2 + x) * W, W), W)
            first[rows, lanes] = src[k, 0].astype(F32)
            second[rows, lanes] = src[k, 1].astype(F32)


AG_ORDER = ((0, 0), (0, 1), (2, 0), (1, 0), (3, 0), (2, 1), (1, 1), (3, 1))


def gather_ch(value):
    other = lax.ppermute(value, "ch", ch_pairs(1, 0))
    near = [lax.ppermute(value, "ch", ch_pairs(0, k)) for k in (1, 3, 2)]
    far = [lax.ppermute(other, "ch", ch_pairs(0, k)) for k in (1, 3, 2)]
    return [value, other, *near, *far]


def scatter_ch(pieces, name):
    far = [lax.ppermute(p, "ch", ch_pairs(0, k)) for k, p in zip((1, 3, 2), pieces[5:8])]
    near = [lax.ppermute(p, "ch", ch_pairs(0, k)) for k, p in zip((1, 3, 2), pieces[2:5])]
    total = sum_four(pieces[1], *far, name=name)
    other = lax.ppermute(total, "ch", ch_pairs(1, 0))
    return [pieces[0], *near, other]


def neighbours(first, last):
    up = [(i, i + 1) for i in range(15)]
    down = [(i + 1, i) for i in range(15)]
    return lax.ppermute(last, "rows", up), lax.ppermute(first, "rows", down)


def sum_rows(value):
    for dz, dx, dc in ((0, 0, 1), (0, 1, 0)):
        value = value + lax.ppermute(value, "rows", row_pairs(dz, dx, dc))
    for bit in (4, 8):
        value = value + lax.ppermute(value, "rows", [(i, i ^ bit) for i in range(16)])
    return value


def final_kernel(p0, p1, p2, p3, p4, out):
    for r in range(ROWS):
        total = p0[r].astype(F32)
        for p in (p1, p2, p3, p4):
            total = total + p[r].astype(F32)
        out[r] = total.astype(BF)


def input_grad(at, grad, wt, name):
    above, below = neighbours(grad[0], grad[ROWS - 1])
    outs = call(
        input_grad_kernel,
        dict(
            shapes=[((STACK, ROWS * W), BF)] + [((ROWS, OWN, W), BF)] * 8,
            scratch=[pltpu.VMEM((3, ROWS + 2, OWN, W), BF), pltpu.VMEM((ROWS, C, W), BF)],
        ),
        at, grad, above, below, wt,
        flops=2 * STACK * C * ROWS * W,
        name=name,
    )
    return outs[0], outs[1:]


def body(x_band, first_filter, second_filter, norm_gain, norm_shift, out_cotangent):
    cells = float((C // G) * ROWS * lax.axis_size("rows") * W)
    ch, rows = lax.axis_index("ch"), lax.axis_index("rows")
    at = jnp.stack([ch // 4, ch % 4, rows // 4, (rows // 2) % 2, rows % 2]).astype(jnp.int32)
    x_rows = jnp.transpose(x_band, (1, 0, 2))
    cot_rows = jnp.transpose(out_cotangent, (1, 0, 2))
    w1 = first_filter.reshape(STACK, C)
    w1t, w2t = w1.T, second_filter.reshape(STACK, C).T
    gain = jnp.broadcast_to(norm_gain[:, None], (OWN, W))
    shift = jnp.broadcast_to(norm_shift[:, None], (OWN, W))
    strip = (ROWS, OWN, W)

    x_pieces = gather_ch(x_rows)
    cot_stack, act_pieces = input_grad(at, cot_rows, w2t, "act_grad")
    hid, top, bottom, x_full = call(
        conv_kernel,
        dict(
            shapes=[(strip, F32), ((OWN, W), F32), ((OWN, W), F32), ((ROWS, C, W), BF)],
            scratch=[pltpu.VMEM((3, ROWS + 2, OWN, W), F32)],
        ),
        at, *x_pieces, w1,
        flops=2 * STACK * C * ROWS * W,
        name="hidden",
    )
    above, below = neighbours(top, bottom)
    hid, stats = call(
        stats_kernel, dict(shapes=[(strip, F32), ((8, W), F32)]), hid, above, below, name="stats"
    )
    act_parts = scatter_ch(act_pieces, "act_grad_sum")
    stats = sum_rows(stats)
    (act,) = call(
        functools.partial(act_kernel, cells), dict(shapes=[(strip, BF)]),
        hid, stats, gain, shift, name="activation",
    )
    pre, sums = call(
        functools.partial(pre_kernel, cells), dict(shapes=[(strip, F32), ((8, W), F32)]),
        hid, stats, gain, shift, *act_parts, name="pre_grad",
    )
    sums = sum_rows(sums)
    act_all = gather_ch(act)
    (hidden_grad,) = call(
        functools.partial(hidden_grad_kernel, cells), dict(shapes=[(strip, BF)]),
        hid, stats, gain, pre, sums, name="hidden_grad",
    )
    half = ((2 * STACK, W), BF)
    keep2, send2 = call(
        gathered_filter_kernel,
        dict(shapes=[half, half], scratch=[pltpu.VMEM((ROWS, C, W), BF)]),
        at, cot_stack, *act_all,
        flops=2 * STACK * C * ROWS * W,
        name="second_grad",
    )
    recv2 = lax.ppermute(send2, "rows", row_pairs(0, 0, 1))
    hg_stack, band_pieces = input_grad(at, hidden_grad, w1t, "band_grad")
    band_parts = scatter_ch(band_pieces, "band_grad_sum")
    keep1, send1 = call(
        filter_kernel, dict(shapes=[half, half]), at, hg_stack, x_full,
        flops=2 * STACK * C * ROWS * W, name="first_grad",
    )
    recv1 = lax.ppermute(send1, "rows", row_pairs(0, 0, 1))
    share = (2, PIECE, W)
    near, far = call(
        core_sum_kernel, dict(shapes=[((4, *share), BF)] * 2), at, keep1, recv1, keep2, recv2, name="core_sum"
    )
    far = lax.ppermute(far, "rows", row_pairs(0, 1, 0))
    zs = call(pair_sum_kernel, dict(shapes=[(share, BF)] * 4), near, far, name="pair_sum")
    got = [lax.ppermute(zs[k], "rows", row_pairs(k, 0, 0)) for k in (2, 1, 3)]
    done = sum_four(zs[0], *got, name="filter_sum")
    other = lax.ppermute(done, "rows", row_pairs(0, 1, 0))
    got = [lax.ppermute(done, "rows", row_pairs(k, 0, 0)) for k in (2, 1, 3)]
    got += [lax.ppermute(other, "rows", row_pairs(k, 0, 0)) for k in (2, 1, 3)]
    mine = jnp.stack([done, other, *got])
    theirs = lax.ppermute(mine, "rows", row_pairs(0, 0, 1))
    first_grad, second_grad = call(
        place_kernel, dict(shapes=[((STACK, C), F32)] * 2), at, mine, theirs, name="filter_grads"
    )
    (band,) = call(final_kernel, dict(shapes=[(strip, BF)]), *band_parts, name="band_grad_total")
    shape = (3, 3, OWN, C)
    return (
        jnp.transpose(band, (1, 0, 2)),
        first_grad.reshape(shape),
        second_grad.reshape(shape),
        sums[0, :OWN],
        sums[0, OWN:],
    )


def solution(mesh):
    filters = P(None, None, "ch", None)
    strip = P("ch", "rows", None)
    return jax.shard_map(
        body,
        mesh=mesh,
        in_specs=(strip, filters, filters, P("ch"), P("ch"), strip),
        out_specs=(strip, filters, filters, P("ch"), P("ch")),
        check_vma=False,
    )
```

```python
import functools

import jax
import jax.numpy as jnp
from jax import lax
from jax.experimental import pallas as pl
from jax.experimental.pallas import tpu as pltpu
from jax.sharding import PartitionSpec as P

C = 512
G = 32
EPS = 1e-06
ROWS = 8
W = 128
OWN = 64
TAPS = 9
STACK = TAPS * OWN
PIECE = 288
BF = jnp.bfloat16
F32 = jnp.float32

VMEM = pl.BlockSpec(memory_space=pltpu.VMEM)
SMEM = pl.BlockSpec(memory_space=pltpu.SMEM)

CH_SHIFTS = ((0, 0), (1, 0), (0, 1), (0, 3), (0, 2), (1, 1), (1, 3), (1, 2))


def after(value, other):
    return lax.optimization_barrier((value, other))[0]


def ch_pairs(dx, dy):
    return [(i, ((i // 4 + dx) % 2) * 4 + (i % 4 + dy) % 4) for i in range(8)]


def row_pairs(dz, dx, dc):
    pairs = []
    for i in range(16):
        z, x, c = i // 4, (i // 2) % 2, i % 2
        pairs.append((i, ((z + dz) % 4) * 4 + ((x + dx) % 2) * 2 + (c + dc) % 2))
    return pairs


GATES = (1, 0, 0, 4, 0, 0)
NG = (3, 0, 0, 0)
HINT = {'act_grad': 21, 'hidden': 26, 'act_grad_sum': 0, 'activation': 0, 'pre_grad': 0, 'second_grad': 0, 'band_grad': 0, 'first_grad': 0, 'band_grad_sum': 0, 'core_sum': 0, 'filter_sum': 0, 'pair_sum': 0, 'own_half': 10, 'other_half': 0, 'band_grad_total': 0}


def hint(name):
    return pl.CostEstimate(flops=int(HINT[name] * 1.15e9), bytes_accessed=0, transcendentals=0)


def call(kernel, out, *args, name=None):
    shapes = [jax.ShapeDtypeStruct(s, d) for s, d in out["shapes"]]
    return pl.pallas_call(
        kernel,
        out_shape=shapes,
        in_specs=[SMEM if a.dtype == jnp.int32 else VMEM for a in args],
        out_specs=[VMEM] * len(shapes),
        scratch_shapes=out.get("scratch", ()),
        compiler_params=pltpu.CompilerParams(vmem_limit_bytes=10 * 1024 * 1024),
        cost_estimate=hint(name),
        name=name,
    )(*args)


def shifted_cols(v, by):
    lane = lax.broadcasted_iota(jnp.int32, v.shape, 1)
    rolled = pltpu.roll(v, by % W, 1)
    return jnp.where(lane == (0 if by == 1 else W - 1), 0.0, rolled)


def source_of(at, shift):
    dx, dy = shift
    return lax.rem(at[0] + dx, 2) * 4 + lax.rem(at[1] + 4 - dy, 4)


def target_of(at, shift):
    dx, dy = shift
    return lax.rem(at[0] + dx, 2) * 4 + lax.rem(at[1] + dy, 4)


def assemble(at, pieces, full):
    for shift, piece in zip(CH_SHIFTS, pieces):
        place = pl.multiple_of(source_of(at, shift) * OWN, OWN)
        full[:, pl.ds(place, OWN), :] = piece[...]


def conv_kernel(at, *refs):
    pieces, (w, hid, stats, full, acc) = refs[:8], refs[8:]
    assemble(at, pieces, full)
    acc[...] = jnp.zeros_like(acc)
    for j in range(ROWS // 2 + 1):
        pair = jnp.concatenate([full[2 * j], full[2 * j + 1]], axis=1)
        v = jnp.dot(w[...], pair, preferred_element_type=F32)
        for a in range(3):
            for b in range(3):
                for k in range(2):
                    o = (a * 3 + b) * OWN
                    y = 2 * j + k - a
                    if 0 <= y < ROWS:
                        acc[b, y] += v[o : o + OWN, k * W : (k + 1) * W]
    total = jnp.zeros((OWN, W), F32)
    square = jnp.zeros((OWN, W), F32)
    for r in range(ROWS):
        row = acc[1, r] + shifted_cols(acc[0, r], 1) + shifted_cols(acc[2, r], -1)
        hid[r] = row
        total = total + row
        square = square + row * row
    both = jnp.concatenate([total, square], axis=0)
    sums = jnp.sum(jnp.sum(both.reshape(8, OWN // 4, W), axis=1), axis=1, keepdims=True)
    stats[...] = jnp.broadcast_to(sums, (8, W))


def per_channel(groups):
    return jnp.broadcast_to(groups[:, None, :], (4, OWN // 4, W)).reshape(OWN, W)


def norm_of(stats, cells):
    mean = stats[0:4] / cells
    var = stats[4:8] / cells - mean * mean
    return per_channel(mean), per_channel(lax.rsqrt(var + EPS))


def act_kernel(cells, hid, stats, gain, shift, act):
    mean, scale = norm_of(stats[...], cells)
    for r in range(ROWS):
        normed = (hid[r] - mean) * scale
        s = normed * gain[...] + shift[...]
        act[r] = (s * jax.nn.sigmoid(s)).astype(BF)


def pre_kernel(cells, hid, stats, gain, shift, near, far, pre, sums):
    mean, scale = norm_of(stats[...], cells)
    by_normed = jnp.zeros((OWN, W), F32)
    plain = jnp.zeros((OWN, W), F32)
    for r in range(ROWS):
        normed = (hid[r] - mean) * scale
        s = normed * gain[...] + shift[...]
        q = jax.nn.sigmoid(s)
        act_grad = near[r] + far[r].astype(F32)
        value = act_grad * q * (1.0 + s * (1.0 - q))
        pre[r] = value
        by_normed = by_normed + value * normed
        plain = plain + value
    both = jnp.concatenate([by_normed, plain], axis=0).T
    sums[...] = jnp.broadcast_to(jnp.sum(both, axis=0, keepdims=True), (8, W))


def shift_columns(r, row, cols):
    wide = row.astype(F32)
    cols[0, r] = shifted_cols(wide, -1).astype(BF)
    cols[1, r] = row
    cols[2, r] = shifted_cols(wide, 1).astype(BF)


def transposed_conv(at, w, stack, pieces, cols, full):
    for j in range(ROWS // 2):
        for a in range(3):
            for b in range(3):
                o = (a * 3 + b) * OWN
                for k in range(2):
                    y = 2 * j + k
                    stack[o : o + OWN, y * W : (y + 1) * W] = cols[b, y - a + 2]
        part = lax.dot_general(
            w[...],
            stack[:, 2 * j * W : (2 * j + 2) * W],
            (((0,), (0,)), ((), ())),
            preferred_element_type=F32,
        ).astype(BF)
        full[2 * j] = part[:, :W]
        full[2 * j + 1] = part[:, W:]
    for k, (near, far) in zip((0, 1, 3, 2), pieces):
        for n, out in enumerate((near, far)):
            place = pl.multiple_of(target_of(at, (n, k)) * OWN, OWN)
            out[...] = full[:, pl.ds(place, OWN), :]


def piece_refs(refs):
    return [(ref.at[0], ref.at[1]) for ref in refs]


def act_grad_kernel(at, grad, above, below, w, stack, *rest):
    pieces, (cols, full) = rest[:4], rest[4:]
    for r in range(ROWS + 2):
        row = above[OWN:] if r == 0 else below[OWN:] if r == ROWS + 1 else grad[r - 1]
        shift_columns(r, row, cols)
    transposed_conv(at, w, stack, piece_refs(pieces), cols, full)


def band_grad_kernel(cells, at, hid, stats, gain, pre, sums, above, below, w, stack, *rest):
    pieces, (cols, full) = rest[:4], rest[4:]
    mean, scale = norm_of(stats[...], cells)
    spread = jnp.broadcast_to(sums[0:1, :], (W, W)).T
    by_normed, plain = spread[:OWN], spread[OWN:]

    def group_mean(v):
        return per_channel(jnp.sum((gain[...] * v).reshape(4, OWN // 4, W), axis=1) / cells)

    first, second = group_mean(plain), group_mean(by_normed)

    def hidden_grad(p, h):
        normed = (h - mean) * scale
        return scale * (p * gain[...] - first - normed * second)

    for r in range(ROWS + 2):
        if r == 0:
            row = jnp.where(at[5] > 0, hidden_grad(above[0], above[1]), 0.0)
        elif r == ROWS + 1:
            row = jnp.where(at[5] < 15, hidden_grad(below[0], below[1]), 0.0)
        else:
            row = hidden_grad(pre[r - 1], hid[r - 1])
        shift_columns(r, row.astype(BF), cols)
    transposed_conv(at, w, stack, piece_refs(pieces), cols, full)


def filter_products(at, stack, full, rows, keep, send):
    for slot, out in enumerate((keep, send)):
        half = lax.rem(at[4] + slot, 2)
        place = pl.ds(pl.multiple_of(half * 2 * W, 2 * W), 2 * W)
        cells = jnp.concatenate([full[r, place, :] for r in rows], axis=1)
        part = lax.dot_general(
            stack[...], cells, (((1,), (1,)), ((), ())), preferred_element_type=F32
        ).astype(BF)
        out[:STACK, :] = part[:, :W]
        out[STACK:, :] = part[:, W:]


def filter_kernel(at, stack, full, keep, send):
    filter_products(at, stack, full, range(1, ROWS + 1), keep, send)


def gathered_filter_kernel(at, stack, *refs):
    pieces, (keep, send, full) = refs[:4], refs[4:]
    for k, piece in zip((0, 1, 3, 2), pieces):
        for n in range(2):
            place = pl.multiple_of(source_of(at, (n, k)) * OWN, OWN)
            full[:, pl.ds(place, OWN), :] = piece[n]
    filter_products(at, stack, full, range(ROWS), keep, send)


def core_sum_kernel(at, k1, r1, k2, r2, *outs):
    for n, (k, r) in enumerate(((k1, r1), (k2, r2))):
        for dz, out in enumerate(outs):
            p = lax.rem(at[2] + dz, 4)
            rows = pl.ds(pl.multiple_of(p * PIECE, PIECE), PIECE)
            out[n] = (k[rows, :].astype(F32) + r[rows, :].astype(F32)).astype(BF)


def two_sum_kernel(a, b, out):
    out[...] = (a[...].astype(F32) + b[...].astype(F32)).astype(BF)


def four_sum_kernel(a, b, c, d, out):
    total = a[...].astype(F32) + b[...].astype(F32) + c[...].astype(F32) + d[...].astype(F32)
    out[...] = total.astype(BF)


def sum_four(a, b, c, d, name):
    return call(four_sum_kernel, dict(shapes=[(a.shape, BF)]), a, b, c, d, name=name)[0]


Z_ORDER = (0, 1, 3, 2)


def place_kernel(half, at, *refs):
    pieces, (first, second, wide, sems) = refs[:4], refs[-4:]
    core = lax.rem(at[4] + half, 2)
    copies = []
    for k, dz in enumerate(Z_ORDER):
        z = lax.rem(at[2] + 4 - dz, 4)
        rows = pl.ds(pl.multiple_of(lax.rem(z, 2) * PIECE, PIECE), PIECE)
        lanes = pl.ds(pl.multiple_of((core * 2 + lax.div(z, 2)) * W, W), W)
        for n, out in enumerate((first, second)):
            wide[k, n] = pieces[k][n].astype(F32)
            copies.append(
                pltpu.make_async_copy(wide.at[k, n], out.at[rows, lanes], sems.at[k, n])
            )
            copies[-1].start()
    for copy in copies:
        copy.wait()


def place(half, at, pieces, outs, name):
    whole = jax.ShapeDtypeStruct((STACK, C), F32)
    anywhere = pl.BlockSpec(memory_space=pl.ANY)
    return pl.pallas_call(
        functools.partial(place_kernel, half),
        out_shape=[whole] * 2,
        in_specs=[SMEM] + [VMEM] * 4 + [anywhere] * len(outs),
        out_specs=[anywhere] * 2,
        input_output_aliases={5 + n: n for n in range(len(outs))},
        scratch_shapes=[pltpu.VMEM((4, 2, PIECE, W), F32), pltpu.SemaphoreType.DMA((4, 2))],
        compiler_params=pltpu.CompilerParams(vmem_limit_bytes=10 * 1024 * 1024),
        cost_estimate=hint(name),
        name=name,
    )(at, *pieces, *outs)


def gather_ch(value):
    other = lax.ppermute(value, "ch", ch_pairs(1, 0))
    near = [lax.ppermute(value, "ch", ch_pairs(0, k)) for k in (1, 3, 2)]
    far = [lax.ppermute(other, "ch", ch_pairs(0, k)) for k in (1, 3, 2)]
    return [value, other, *near, *far]


def gather_ch_pairs(value):
    both = jnp.stack([value, lax.ppermute(value, "ch", ch_pairs(1, 0))])
    return [both] + [lax.ppermute(both, "ch", ch_pairs(0, k)) for k in (1, 3, 2)]


def scatter_sum_kernel(own, a, b, c, near, far):
    for n, out in enumerate((near, far)):
        total = own[n].astype(F32) + a[n].astype(F32) + b[n].astype(F32) + c[n].astype(F32)
        out[...] = total.astype(out.dtype)


def scatter_ch(pieces, name, gate=None):
    got = [lax.ppermute(p, "ch", ch_pairs(0, k)) for k, p in zip((1, 3, 2), pieces[1:])]
    own = pieces[0] if gate is None else after(pieces[0], gate)
    near, far = call(
        scatter_sum_kernel, dict(shapes=[((ROWS, OWN, W), F32), ((ROWS, OWN, W), BF)]),
        own, *got, name=name,
    )
    return near, lax.ppermute(far, "ch", ch_pairs(1, 0)), got


def neighbours(first, last):
    up = [(i, i + 1) for i in range(15)]
    down = [(i + 1, i) for i in range(15)]
    return lax.ppermute(last, "rows", up), lax.ppermute(first, "rows", down)


def sum_rows_near(value):
    for dz, dx, dc in ((0, 0, 1), (0, 1, 0)):
        value = value + lax.ppermute(value, "rows", row_pairs(dz, dx, dc))
    return value


def sum_rows_far(value, gate=None):
    for mask in (4, 8):
        if mask == 8 and gate is not None:
            value = after(value, gate)
        value = value + lax.ppermute(value, "rows", [(i, i ^ mask) for i in range(16)])
    return value


def final_kernel(near, far, out):
    for r in range(ROWS):
        out[r] = (near[r] + far[r].astype(F32)).astype(BF)


def input_grad(kernel, w, *args, name):
    outs = call(
        kernel,
        dict(
            shapes=[((STACK, ROWS * W), BF)] + [((2, ROWS, OWN, W), BF)] * 4,
            scratch=[pltpu.VMEM((3, ROWS + 2, OWN, W), BF), pltpu.VMEM((ROWS, C, W), BF)],
        ),
        *args, w,
        name=name,
    )
    return outs[0], outs[1:]


def body(x_band, first_filter, second_filter, norm_gain, norm_shift, out_cotangent):
    cells = float((C // G) * ROWS * lax.axis_size("rows") * W)
    ch, rows = lax.axis_index("ch"), lax.axis_index("rows")
    at = jnp.stack([ch // 4, ch % 4, rows // 4, (rows // 2) % 2, rows % 2, rows]).astype(jnp.int32)
    x_band, out_cotangent, at = lax.optimization_barrier((x_band, out_cotangent, at))
    x_above, x_below = neighbours(
        *(jnp.concatenate([x_band[:, r], out_cotangent[:, r]]) for r in (0, ROWS - 1))
    )
    cot_rows = jnp.transpose(out_cotangent, (1, 0, 2))
    x_rows = jnp.concatenate(
        [x_above[None, :OWN], jnp.transpose(x_band, (1, 0, 2)), x_below[None, :OWN]]
    )
    w1 = first_filter.reshape(STACK, C)
    w2 = second_filter.reshape(STACK, C)
    gain = jnp.broadcast_to(norm_gain[:, None], (OWN, W))
    shift = jnp.broadcast_to(norm_shift[:, None], (OWN, W))
    strip = (ROWS, OWN, W)

    x_pieces = gather_ch(x_rows)
    cot_stack, act_pieces = input_grad(
        act_grad_kernel, w2, at, after(cot_rows, x_pieces[GATES[3]]), x_above, x_below, name="act_grad"
    )
    hid, stats, x_full = call(
        conv_kernel,
        dict(
            shapes=[(strip, F32), ((8, W), F32), ((ROWS + 2, C, W), BF)],
            scratch=[pltpu.VMEM((3, ROWS, OWN, W), F32)],
        ),
        at, *x_pieces, w1,
        name="hidden",
    )
    stats = sum_rows_near(stats)
    *act_parts, _ = scatter_ch([after(p, x_pieces[GATES[5]]) if GATES[5] else p for p in act_pieces], "act_grad_sum", stats)
    stats = sum_rows_far(stats, act_parts[0] if GATES[0] else None)
    (act,) = call(
        functools.partial(act_kernel, cells), dict(shapes=[(strip, BF)]),
        hid, stats, gain, shift, name="activation",
    )
    pre, sums = call(
        functools.partial(pre_kernel, cells), dict(shapes=[(strip, F32), ((8, W), F32)]),
        hid, stats, gain, shift, *act_parts, name="pre_grad",
    )
    act_all = gather_ch_pairs(act)
    sums = sum_rows_near(sums)
    if GATES[1] == 2:
        sums = after(sums, act_all[0])
    sums = sum_rows_far(sums, act_all[0] if GATES[1] == 1 else None)
    above, below = neighbours(
        jnp.stack([pre[0], hid[0]]), jnp.stack([pre[ROWS - 1], hid[ROWS - 1]])
    )
    half = ((2 * STACK, W), BF)
    hg_stack, band_pieces = input_grad(
        functools.partial(band_grad_kernel, cells), w1,
        at, hid, stats, gain, pre, after(sums, act_all[1 : 1 + NG[0]]) if NG[0] else sums, above, below,
        name="band_grad",
    )
    *band_parts, band_got = scatter_ch(band_pieces, "band_grad_sum")
    keep1, send1 = call(
        filter_kernel, dict(shapes=[half, half]), at, hg_stack, x_full,
        name="first_grad",
    )
    recv1 = lax.ppermute(send1, "rows", row_pairs(0, 0, 1))
    keep2, send2 = call(
        gathered_filter_kernel,
        dict(shapes=[half, half], scratch=[pltpu.VMEM((ROWS, C, W), BF)]),
        at, cot_stack if GATES[4] == 0 else after(cot_stack, hg_stack if GATES[4] == 1 else keep1), *act_all,
        name="second_grad",
    )
    recv2 = lax.ppermute(send2, "rows", row_pairs(0, 0, 1))
    share = ((2, PIECE, W), BF)
    parts = call(
        core_sum_kernel, dict(shapes=[share] * 4), at, after(keep1, band_got[0]) if NG[1] else keep1, recv1, keep2, recv2, name="core_sum"
    )
    got = [lax.ppermute(parts[k], "rows", row_pairs(k, 0, 0)) for k in (1, 3, 2)]
    gain_grad, shift_grad = sums[0, :OWN], sums[0, OWN:]
    part = sum_four(after(parts[0], (gain_grad, shift_grad, *band_parts[: NG[2]])), *got, name="filter_sum")
    part = call(
        two_sum_kernel, dict(shapes=[share]),
        part, lax.ppermute(after(part, band_parts[0]) if GATES[2] == 1 else part, "rows", row_pairs(0, 1, 0)), name="pair_sum",
    )[0]
    if NG[3]:
        part = after(part, band_parts[1])
    mine = [part] + [lax.ppermute(part, "rows", row_pairs(k, 0, 0)) for k in Z_ORDER[1:]]
    theirs = [lax.ppermute(p, "rows", row_pairs(0, 0, 1)) for p in mine]
    grads = place(0, at, mine, (), "own_half")
    first_grad, second_grad = place(1, at, theirs, grads, "other_half")
    (band,) = call(final_kernel, dict(shapes=[(strip, BF)]), *band_parts, name="band_grad_total")
    shape = (3, 3, OWN, C)
    return (
        jnp.transpose(band, (1, 0, 2)),
        first_grad.reshape(shape),
        second_grad.reshape(shape),
        gain_grad,
        shift_grad,
    )


def solution(mesh):
    filters = P(None, None, "ch", None)
    strip = P("ch", "rows", None)
    return jax.shard_map(
        body,
        mesh=mesh,
        in_specs=(strip, filters, filters, P("ch"), P("ch"), strip),
        out_specs=(strip, filters, filters, P("ch"), P("ch")),
        check_vma=False,
    )
```

```python
import functools

import jax
import jax.numpy as jnp
from jax import lax
from jax.experimental import pallas as pl
from jax.experimental.pallas import tpu as pltpu
from jax.sharding import PartitionSpec as P

C = 512
G = 32
EPS = 1e-06
ROWS = 8
W = 128
OWN = 64
TAPS = 9
STACK = TAPS * OWN
PIECE = 288
BF = jnp.bfloat16
F32 = jnp.float32

VMEM = pl.BlockSpec(memory_space=pltpu.VMEM)
SMEM = pl.BlockSpec(memory_space=pltpu.SMEM)

CH_SHIFTS = ((0, 0), (1, 0), (0, 1), (0, 3), (0, 2), (1, 1), (1, 3), (1, 2))


def after(value, other):
    return lax.optimization_barrier((value, other))[0]


def ch_pairs(dx, dy):
    return [(i, ((i // 4 + dx) % 2) * 4 + (i % 4 + dy) % 4) for i in range(8)]


def row_pairs(dz, dx, dc):
    pairs = []
    for i in range(16):
        z, x, c = i // 4, (i // 2) % 2, i % 2
        pairs.append((i, ((z + dz) % 4) * 4 + ((x + dx) % 2) * 2 + (c + dc) % 2))
    return pairs


HINT = {'act_grad': 0, 'hidden': 26, 'act_grad_sum': 0, 'activation': 0, 'pre_grad': 0, 'second_grad': 0, 'band_grad': 0, 'first_grad': 0, 'band_grad_sum': 0, 'core_sum': 0, 'filter_sum': 25, 'pair_sum': 0, 'own_half': 10, 'other_half': 0, 'band_grad_total': 0}


def hint(name):
    return pl.CostEstimate(flops=int(HINT[name] * 1.15e9), bytes_accessed=0, transcendentals=0)


def call(kernel, out, *args, name=None):
    shapes = [jax.ShapeDtypeStruct(s, d) for s, d in out["shapes"]]
    return pl.pallas_call(
        kernel,
        out_shape=shapes,
        in_specs=[SMEM if a.dtype == jnp.int32 else VMEM for a in args],
        out_specs=[VMEM] * len(shapes),
        scratch_shapes=out.get("scratch", ()),
        compiler_params=pltpu.CompilerParams(vmem_limit_bytes=10 * 1024 * 1024),
        cost_estimate=hint(name),
        name=name,
    )(*args)


def shifted_cols(v, by):
    lane = lax.broadcasted_iota(jnp.int32, v.shape, 1)
    rolled = pltpu.roll(v, by % W, 1)
    return jnp.where(lane == (0 if by == 1 else W - 1), 0.0, rolled)


def source_of(at, shift):
    dx, dy = shift
    return lax.rem(at[0] + dx, 2) * 4 + lax.rem(at[1] + 4 - dy, 4)


def target_of(at, shift):
    dx, dy = shift
    return lax.rem(at[0] + dx, 2) * 4 + lax.rem(at[1] + dy, 4)


def assemble(at, pieces, full):
    for shift, piece in zip(CH_SHIFTS, pieces):
        place = pl.multiple_of(source_of(at, shift) * OWN, OWN)
        full[:, pl.ds(place, OWN), :] = piece[...]


def conv_kernel(at, *refs):
    pieces, (w, hid, stats, full, acc) = refs[:8], refs[8:]
    assemble(at, pieces, full)
    acc[...] = jnp.zeros_like(acc)
    for j in range(ROWS // 2 + 1):
        pair = jnp.concatenate([full[2 * j], full[2 * j + 1]], axis=1)
        v = jnp.dot(w[...], pair, preferred_element_type=F32)
        for a in range(3):
            for b in range(3):
                for k in range(2):
                    o = (a * 3 + b) * OWN
                    y = 2 * j + k - a
                    if 0 <= y < ROWS:
                        acc[b, y] += v[o : o + OWN, k * W : (k + 1) * W]
    total = jnp.zeros((OWN, W), F32)
    square = jnp.zeros((OWN, W), F32)
    for r in range(ROWS):
        row = acc[1, r] + shifted_cols(acc[0, r], 1) + shifted_cols(acc[2, r], -1)
        hid[r] = row
        total = total + row
        square = square + row * row
    both = jnp.concatenate([total, square], axis=0)
    sums = jnp.sum(jnp.sum(both.reshape(8, OWN // 4, W), axis=1), axis=1, keepdims=True)
    stats[...] = jnp.broadcast_to(sums, (8, W))


def per_channel(groups):
    return jnp.broadcast_to(groups[:, None, :], (4, OWN // 4, W)).reshape(OWN, W)


def norm_of(stats, cells):
    mean = stats[0:4] / cells
    var = stats[4:8] / cells - mean * mean
    return per_channel(mean), per_channel(lax.rsqrt(var + EPS))


def act_kernel(cells, hid, stats, gain, shift, act):
    mean, scale = norm_of(stats[...], cells)
    for r in range(ROWS):
        normed = (hid[r] - mean) * scale
        s = normed * gain[...] + shift[...]
        act[r] = (s * jax.nn.sigmoid(s)).astype(BF)


def pre_kernel(cells, hid, stats, gain, shift, near, far, pre, sums):
    mean, scale = norm_of(stats[...], cells)
    by_normed = jnp.zeros((OWN, W), F32)
    plain = jnp.zeros((OWN, W), F32)
    for r in range(ROWS):
        normed = (hid[r] - mean) * scale
        s = normed * gain[...] + shift[...]
        q = jax.nn.sigmoid(s)
        act_grad = near[r] + far[r].astype(F32)
        value = act_grad * q * (1.0 + s * (1.0 - q))
        pre[r] = value
        by_normed = by_normed + value * normed
        plain = plain + value
    both = jnp.concatenate([by_normed, plain], axis=0).T
    sums[...] = jnp.broadcast_to(jnp.sum(both, axis=0, keepdims=True), (8, W))


def shift_columns(r, row, cols):
    wide = row.astype(F32)
    cols[0, r] = shifted_cols(wide, -1).astype(BF)
    cols[1, r] = row
    cols[2, r] = shifted_cols(wide, 1).astype(BF)


def transposed_conv(at, w, stack, pieces, cols, full):
    for j in range(ROWS // 2):
        for a in range(3):
            for b in range(3):
                o = (a * 3 + b) * OWN
                for k in range(2):
                    y = 2 * j + k
                    stack[o : o + OWN, y * W : (y + 1) * W] = cols[b, y - a + 2]
        part = lax.dot_general(
            w[...],
            stack[:, 2 * j * W : (2 * j + 2) * W],
            (((0,), (0,)), ((), ())),
            preferred_element_type=F32,
        ).astype(BF)
        full[2 * j] = part[:, :W]
        full[2 * j + 1] = part[:, W:]
    for k, (near, far) in zip((0, 1, 3, 2), pieces):
        for n, out in enumerate((near, far)):
            place = pl.multiple_of(target_of(at, (n, k)) * OWN, OWN)
            out[...] = full[:, pl.ds(place, OWN), :]


def piece_refs(refs):
    return [(ref.at[0], ref.at[1]) for ref in refs]


def act_grad_kernel(at, grad, above, below, w, stack, *rest):
    pieces, (cols, full) = rest[:4], rest[4:]
    for r in range(ROWS + 2):
        row = above[OWN:] if r == 0 else below[OWN:] if r == ROWS + 1 else grad[r - 1]
        shift_columns(r, row, cols)
    transposed_conv(at, w, stack, piece_refs(pieces), cols, full)


def band_grad_kernel(cells, at, hid, stats, gain, pre, sums, above, below, w, stack, *rest):
    pieces, (cols, full) = rest[:4], rest[4:]
    mean, scale = norm_of(stats[...], cells)
    spread = jnp.broadcast_to(sums[0:1, :], (W, W)).T
    by_normed, plain = spread[:OWN], spread[OWN:]

    def group_mean(v):
        return per_channel(jnp.sum((gain[...] * v).reshape(4, OWN // 4, W), axis=1) / cells)

    first, second = group_mean(plain), group_mean(by_normed)

    def hidden_grad(p, h):
        normed = (h - mean) * scale
        return scale * (p * gain[...] - first - normed * second)

    for r in range(ROWS + 2):
        if r == 0:
            row = jnp.where(at[5] > 0, hidden_grad(above[0], above[1]), 0.0)
        elif r == ROWS + 1:
            row = jnp.where(at[5] < 15, hidden_grad(below[0], below[1]), 0.0)
        else:
            row = hidden_grad(pre[r - 1], hid[r - 1])
        shift_columns(r, row.astype(BF), cols)
    transposed_conv(at, w, stack, piece_refs(pieces), cols, full)


def filter_products(at, stack, full, rows, keep, send):
    for slot, out in enumerate((keep, send)):
        half = lax.rem(at[4] + slot, 2)
        place = pl.ds(pl.multiple_of(half * 2 * W, 2 * W), 2 * W)
        cells = jnp.concatenate([full[r, place, :] for r in rows], axis=1)
        part = lax.dot_general(
            stack[...], cells, (((1,), (1,)), ((), ())), preferred_element_type=F32
        ).astype(BF)
        out[:STACK, :] = part[:, :W]
        out[STACK:, :] = part[:, W:]


def filter_kernel(at, stack, full, keep, send):
    filter_products(at, stack, full, range(1, ROWS + 1), keep, send)


def gathered_filter_kernel(at, stack, *refs):
    pieces, (keep, send, full) = refs[:4], refs[4:]
    for k, piece in zip((0, 1, 3, 2), pieces):
        for n in range(2):
            place = pl.multiple_of(source_of(at, (n, k)) * OWN, OWN)
            full[:, pl.ds(place, OWN), :] = piece[n]
    filter_products(at, stack, full, range(ROWS), keep, send)


def core_sum_kernel(at, k1, r1, k2, r2, *outs):
    for n, (k, r) in enumerate(((k1, r1), (k2, r2))):
        for dz, out in enumerate(outs):
            p = lax.rem(at[2] + dz, 4)
            rows = pl.ds(pl.multiple_of(p * PIECE, PIECE), PIECE)
            out[n] = (k[rows, :].astype(F32) + r[rows, :].astype(F32)).astype(BF)


def two_sum_kernel(a, b, out):
    out[...] = (a[...].astype(F32) + b[...].astype(F32)).astype(BF)


def four_sum_kernel(a, b, c, d, out):
    total = a[...].astype(F32) + b[...].astype(F32) + c[...].astype(F32) + d[...].astype(F32)
    out[...] = total.astype(BF)


def sum_four(a, b, c, d, name):
    return call(four_sum_kernel, dict(shapes=[(a.shape, BF)]), a, b, c, d, name=name)[0]


Z_ORDER = (0, 1, 3, 2)


def place_kernel(half, at, *refs):
    pieces, (first, second, wide, sems) = refs[:4], refs[-4:]
    core = lax.rem(at[4] + half, 2)
    copies = []
    for k, dz in enumerate(Z_ORDER):
        z = lax.rem(at[2] + 4 - dz, 4)
        rows = pl.ds(pl.multiple_of(lax.rem(z, 2) * PIECE, PIECE), PIECE)
        lanes = pl.ds(pl.multiple_of((core * 2 + lax.div(z, 2)) * W, W), W)
        for n, out in enumerate((first, second)):
            wide[k, n] = pieces[k][n].astype(F32)
            copies.append(
                pltpu.make_async_copy(wide.at[k, n], out.at[rows, lanes], sems.at[k, n])
            )
            copies[-1].start()
    for copy in copies:
        copy.wait()


def place(half, at, pieces, outs, name):
    whole = jax.ShapeDtypeStruct((STACK, C), F32)
    anywhere = pl.BlockSpec(memory_space=pl.ANY)
    return pl.pallas_call(
        functools.partial(place_kernel, half),
        out_shape=[whole] * 2,
        in_specs=[SMEM] + [VMEM] * 4 + [anywhere] * len(outs),
        out_specs=[anywhere] * 2,
        input_output_aliases={5 + n: n for n in range(len(outs))},
        scratch_shapes=[pltpu.VMEM((4, 2, PIECE, W), F32), pltpu.SemaphoreType.DMA((4, 2))],
        compiler_params=pltpu.CompilerParams(vmem_limit_bytes=10 * 1024 * 1024),
        cost_estimate=hint(name),
        name=name,
    )(at, *pieces, *outs)


def gather_ch(value):
    other = lax.ppermute(value, "ch", ch_pairs(1, 0))
    near = [lax.ppermute(value, "ch", ch_pairs(0, k)) for k in (1, 3, 2)]
    far = [lax.ppermute(other, "ch", ch_pairs(0, k)) for k in (1, 3, 2)]
    return [value, other, *near, *far]


def gather_ch_pairs(value):
    both = jnp.stack([value, lax.ppermute(value, "ch", ch_pairs(1, 0))])
    return [both] + [lax.ppermute(both, "ch", ch_pairs(0, k)) for k in (1, 3, 2)]


def scatter_sum_kernel(own, a, b, c, near, far):
    for n, out in enumerate((near, far)):
        total = own[n].astype(F32) + a[n].astype(F32) + b[n].astype(F32) + c[n].astype(F32)
        out[...] = total.astype(out.dtype)


def scatter_ch(pieces, name, gate=None):
    got = [lax.ppermute(p, "ch", ch_pairs(0, k)) for k, p in zip((1, 3, 2), pieces[1:])]
    own = pieces[0] if gate is None else after(pieces[0], gate)
    near, far = call(
        scatter_sum_kernel, dict(shapes=[((ROWS, OWN, W), F32), ((ROWS, OWN, W), BF)]),
        own, *got, name=name,
    )
    return near, lax.ppermute(far, "ch", ch_pairs(1, 0)), got


def neighbours(first, last):
    up = [(i, i + 1) for i in range(15)]
    down = [(i + 1, i) for i in range(15)]
    return lax.ppermute(last, "rows", up), lax.ppermute(first, "rows", down)


def sum_rows_near(value):
    for dz, dx, dc in ((0, 0, 1), (0, 1, 0)):
        value = value + lax.ppermute(value, "rows", row_pairs(dz, dx, dc))
    return value


def sum_rows_far(value, gate=None):
    for mask in (4, 8):
        if mask == 8 and gate is not None:
            value = after(value, gate)
        value = value + lax.ppermute(value, "rows", [(i, i ^ mask) for i in range(16)])
    return value


def final_kernel(near, far, out):
    for r in range(ROWS):
        out[r] = (near[r] + far[r].astype(F32)).astype(BF)


def input_grad(kernel, w, *args, name):
    outs = call(
        kernel,
        dict(
            shapes=[((STACK, ROWS * W), BF)] + [((2, ROWS, OWN, W), BF)] * 4,
            scratch=[pltpu.VMEM((3, ROWS + 2, OWN, W), BF), pltpu.VMEM((ROWS, C, W), BF)],
        ),
        *args, w,
        name=name,
    )
    return outs[0], outs[1:]


def body(x_band, first_filter, second_filter, norm_gain, norm_shift, out_cotangent):
    cells = float((C // G) * ROWS * lax.axis_size("rows") * W)
    ch, rows = lax.axis_index("ch"), lax.axis_index("rows")
    at = jnp.stack([ch // 4, ch % 4, rows // 4, (rows // 2) % 2, rows % 2, rows]).astype(jnp.int32)
    x_band, out_cotangent, at = lax.optimization_barrier((x_band, out_cotangent, at))
    x_above, x_below = neighbours(
        *(jnp.concatenate([x_band[:, r], out_cotangent[:, r]]) for r in (0, ROWS - 1))
    )
    cot_rows = jnp.transpose(out_cotangent, (1, 0, 2))
    x_rows = jnp.concatenate(
        [x_above[None, :OWN], jnp.transpose(x_band, (1, 0, 2)), x_below[None, :OWN]]
    )
    w1 = first_filter.reshape(STACK, C)
    w2 = second_filter.reshape(STACK, C)
    gain = jnp.broadcast_to(norm_gain[:, None], (OWN, W))
    shift = jnp.broadcast_to(norm_shift[:, None], (OWN, W))
    strip = (ROWS, OWN, W)

    x_pieces = gather_ch(x_rows)
    cot_stack, act_pieces = input_grad(
        act_grad_kernel, w2, at, after(cot_rows, x_pieces[4]), x_above, x_below, name="act_grad"
    )
    hid, stats, x_full = call(
        conv_kernel,
        dict(
            shapes=[(strip, F32), ((8, W), F32), ((ROWS + 2, C, W), BF)],
            scratch=[pltpu.VMEM((3, ROWS, OWN, W), F32)],
        ),
        at, *x_pieces, w1,
        name="hidden",
    )
    stats = sum_rows_near(stats)
    *act_parts, _ = scatter_ch(act_pieces, "act_grad_sum", stats)
    stats = sum_rows_far(stats, act_parts[0])
    (act,) = call(
        functools.partial(act_kernel, cells), dict(shapes=[(strip, BF)]),
        hid, stats, gain, shift, name="activation",
    )
    pre, sums = call(
        functools.partial(pre_kernel, cells), dict(shapes=[(strip, F32), ((8, W), F32)]),
        hid, stats, gain, shift, *act_parts, name="pre_grad",
    )
    act_all = gather_ch_pairs(act)
    sums = sum_rows_near(sums)
    sums = after(sums, act_all[0])
    sums = sum_rows_far(sums)
    above, below = neighbours(
        jnp.stack([pre[0], hid[0]]), jnp.stack([pre[ROWS - 1], hid[ROWS - 1]])
    )
    half = ((2 * STACK, W), BF)
    hg_stack, band_pieces = input_grad(
        functools.partial(band_grad_kernel, cells), w1,
        at, hid, stats, gain, pre, after(sums, act_all[1:3]), above, below,
        name="band_grad",
    )
    keep1, send1 = call(
        filter_kernel, dict(shapes=[half, half]), at, hg_stack, x_full,
        name="first_grad",
    )
    recv1 = lax.ppermute(send1, "rows", row_pairs(0, 0, 1))
    keep2, send2 = call(
        gathered_filter_kernel,
        dict(shapes=[half, half], scratch=[pltpu.VMEM((ROWS, C, W), BF)]),
        at, cot_stack, *act_all,
        name="second_grad",
    )
    recv2 = lax.ppermute(send2, "rows", row_pairs(0, 0, 1))
    share = ((2, PIECE, W), BF)
    parts = call(
        core_sum_kernel, dict(shapes=[share] * 4), at, keep1, recv1, keep2, recv2, name="core_sum"
    )
    got = [lax.ppermute(parts[k], "rows", row_pairs(k, 0, 0)) for k in (1, 3, 2)]
    *band_parts, band_got = scatter_ch([after(p, parts[0]) for p in band_pieces], "band_grad_sum")
    gain_grad, shift_grad = sums[0, :OWN], sums[0, OWN:]
    part = sum_four(after(parts[0], (gain_grad, shift_grad)), *got, name="filter_sum")
    part = call(
        two_sum_kernel, dict(shapes=[share]),
        part, lax.ppermute(part, "rows", row_pairs(0, 1, 0)), name="pair_sum",
    )[0]
    mine = [part] + [lax.ppermute(part, "rows", row_pairs(k, 0, 0)) for k in Z_ORDER[1:]]
    theirs = [lax.ppermute(p, "rows", row_pairs(0, 0, 1)) for p in mine]
    grads = place(0, at, mine, (), "own_half")
    first_grad, second_grad = place(1, at, theirs, grads, "other_half")
    (band,) = call(final_kernel, dict(shapes=[(strip, BF)]), *band_parts, name="band_grad_total")
    shape = (3, 3, OWN, C)
    return (
        jnp.transpose(band, (1, 0, 2)),
        first_grad.reshape(shape),
        second_grad.reshape(shape),
        gain_grad,
        shift_grad,
    )


def solution(mesh):
    filters = P(None, None, "ch", None)
    strip = P("ch", "rows", None)
    return jax.shard_map(
        body,
        mesh=mesh,
        in_specs=(strip, filters, filters, P("ch"), P("ch"), strip),
        out_specs=(strip, filters, filters, P("ch"), P("ch")),
        check_vma=False,
    )
```

```python
import functools

import jax
import jax.numpy as jnp
from jax import lax
from jax.experimental import pallas as pl
from jax.experimental.pallas import tpu as pltpu
from jax.sharding import PartitionSpec as P

C = 512
G = 32
EPS = 1e-06
ROWS = 8
W = 128
OWN = 64
TAPS = 9
STACK = TAPS * OWN
PIECE = 288
BF = jnp.bfloat16
F32 = jnp.float32

VMEM = pl.BlockSpec(memory_space=pltpu.VMEM)
SMEM = pl.BlockSpec(memory_space=pltpu.SMEM)

CH_SHIFTS = ((0, 0), (1, 0), (0, 1), (0, 3), (0, 2), (1, 1), (1, 3), (1, 2))


def after(value, other):
    return lax.optimization_barrier((value, other))[0]


def ch_pairs(dx, dy):
    return [(i, ((i // 4 + dx) % 2) * 4 + (i % 4 + dy) % 4) for i in range(8)]


def row_pairs(dz, dx, dc):
    pairs = []
    for i in range(16):
        z, x, c = i // 4, (i // 2) % 2, i % 2
        pairs.append((i, ((z + dz) % 4) * 4 + ((x + dx) % 2) * 2 + (c + dc) % 2))
    return pairs


HINT = {'act_grad': 0, 'hidden': 26, 'act_grad_sum': 0, 'activation': 0, 'pre_grad': 0, 'second_grad': 0, 'band_grad': 0, 'first_grad': 0, 'band_grad_sum': 0, 'core_sum': 0, 'filter_sum': 25, 'pair_sum': 0, 'own_half': 10, 'other_half': 0, 'band_grad_total': 0}


def hint(name):
    return pl.CostEstimate(flops=int(HINT[name] * 1.15e9), bytes_accessed=0, transcendentals=0)


def call(kernel, out, *args, name=None):
    shapes = [jax.ShapeDtypeStruct(s, d) for s, d in out["shapes"]]
    return pl.pallas_call(
        kernel,
        out_shape=shapes,
        in_specs=[SMEM if a.dtype == jnp.int32 else VMEM for a in args],
        out_specs=[VMEM] * len(shapes),
        scratch_shapes=out.get("scratch", ()),
        compiler_params=pltpu.CompilerParams(vmem_limit_bytes=10 * 1024 * 1024),
        cost_estimate=hint(name),
        name=name,
    )(*args)


def shifted_cols(v, by):
    lane = lax.broadcasted_iota(jnp.int32, v.shape, 1)
    rolled = pltpu.roll(v, by % W, 1)
    return jnp.where(lane == (0 if by == 1 else W - 1), 0.0, rolled)


def source_of(at, shift):
    dx, dy = shift
    return lax.rem(at[0] + dx, 2) * 4 + lax.rem(at[1] + 4 - dy, 4)


def target_of(at, shift):
    dx, dy = shift
    return lax.rem(at[0] + dx, 2) * 4 + lax.rem(at[1] + dy, 4)


def assemble(at, pieces, full):
    for shift, piece in zip(CH_SHIFTS, pieces):
        place = pl.multiple_of(source_of(at, shift) * OWN, OWN)
        full[:, pl.ds(place, OWN), :] = piece[...]


def conv_kernel(at, *refs):
    pieces, (w, hid, stats, full, acc) = refs[:8], refs[8:]
    assemble(at, pieces, full)
    acc[...] = jnp.zeros_like(acc)
    for j in range(ROWS // 2 + 1):
        pair = jnp.concatenate([full[2 * j], full[2 * j + 1]], axis=1)
        v = jnp.dot(w[...], pair, preferred_element_type=F32)
        for a in range(3):
            for b in range(3):
                for k in range(2):
                    o = (a * 3 + b) * OWN
                    y = 2 * j + k - a
                    if 0 <= y < ROWS:
                        acc[b, y] += v[o : o + OWN, k * W : (k + 1) * W]
    total = jnp.zeros((OWN, W), F32)
    square = jnp.zeros((OWN, W), F32)
    for r in range(ROWS):
        row = acc[1, r] + shifted_cols(acc[0, r], 1) + shifted_cols(acc[2, r], -1)
        hid[r] = row
        total = total + row
        square = square + row * row
    both = jnp.concatenate([total, square], axis=0)
    sums = jnp.sum(jnp.sum(both.reshape(8, OWN // 4, W), axis=1), axis=1, keepdims=True)
    stats[...] = jnp.broadcast_to(sums, (8, W))


def per_channel(groups):
    return jnp.broadcast_to(groups[:, None, :], (4, OWN // 4, W)).reshape(OWN, W)


def norm_of(stats, cells):
    mean = stats[0:4] / cells
    var = stats[4:8] / cells - mean * mean
    return per_channel(mean), per_channel(lax.rsqrt(var + EPS))


def act_kernel(cells, hid, stats, gain, shift, act):
    mean, scale = norm_of(stats[...], cells)
    for r in range(ROWS):
        normed = (hid[r] - mean) * scale
        s = normed * gain[...] + shift[...]
        act[r] = (s * jax.nn.sigmoid(s)).astype(BF)


def pre_kernel(cells, hid, stats, gain, shift, near, far, pre, sums):
    mean, scale = norm_of(stats[...], cells)
    by_normed = jnp.zeros((OWN, W), F32)
    plain = jnp.zeros((OWN, W), F32)
    for r in range(ROWS):
        normed = (hid[r] - mean) * scale
        s = normed * gain[...] + shift[...]
        q = jax.nn.sigmoid(s)
        act_grad = near[r] + far[r].astype(F32)
        value = act_grad * q * (1.0 + s * (1.0 - q))
        pre[r] = value
        by_normed = by_normed + value * normed
        plain = plain + value
    both = jnp.concatenate([by_normed, plain], axis=0).T
    sums[...] = jnp.broadcast_to(jnp.sum(both, axis=0, keepdims=True), (8, W))


def shift_columns(r, row, cols):
    wide = row.astype(F32)
    cols[0, r] = shifted_cols(wide, -1).astype(BF)
    cols[1, r] = row
    cols[2, r] = shifted_cols(wide, 1).astype(BF)


def transposed_conv(at, w, stack, pieces, cols, full):
    for j in range(ROWS // 2):
        for a in range(3):
            for b in range(3):
                o = (a * 3 + b) * OWN
                for k in range(2):
                    y = 2 * j + k
                    stack[o : o + OWN, y * W : (y + 1) * W] = cols[b, y - a + 2]
        part = lax.dot_general(
            w[...],
            stack[:, 2 * j * W : (2 * j + 2) * W],
            (((0,), (0,)), ((), ())),
            preferred_element_type=F32,
        ).astype(BF)
        full[2 * j] = part[:, :W]
        full[2 * j + 1] = part[:, W:]
    for k, (near, far) in zip((0, 1, 3, 2), pieces):
        for n, out in enumerate((near, far)):
            place = pl.multiple_of(target_of(at, (n, k)) * OWN, OWN)
            out[...] = full[:, pl.ds(place, OWN), :]


def piece_refs(refs):
    return [(ref.at[0], ref.at[1]) for ref in refs]


def act_grad_kernel(at, grad, above, below, w, stack, *rest):
    pieces, (cols, full) = rest[:4], rest[4:]
    for r in range(ROWS + 2):
        row = above[OWN:] if r == 0 else below[OWN:] if r == ROWS + 1 else grad[r - 1]
        shift_columns(r, row, cols)
    transposed_conv(at, w, stack, piece_refs(pieces), cols, full)


def band_grad_kernel(cells, at, hid, stats, gain, pre, sums, above, below, w, stack, *rest):
    pieces, (cols, full) = rest[:4], rest[4:]
    mean, scale = norm_of(stats[...], cells)
    spread = jnp.broadcast_to(sums[0:1, :], (W, W)).T
    by_normed, plain = spread[:OWN], spread[OWN:]

    def group_mean(v):
        return per_channel(jnp.sum((gain[...] * v).reshape(4, OWN // 4, W), axis=1) / cells)

    first, second = group_mean(plain), group_mean(by_normed)

    def hidden_grad(p, h):
        normed = (h - mean) * scale
        return scale * (p * gain[...] - first - normed * second)

    for r in range(ROWS + 2):
        if r == 0:
            row = jnp.where(at[5] > 0, hidden_grad(above[0], above[1]), 0.0)
        elif r == ROWS + 1:
            row = jnp.where(at[5] < 15, hidden_grad(below[0], below[1]), 0.0)
        else:
            row = hidden_grad(pre[r - 1], hid[r - 1])
        shift_columns(r, row.astype(BF), cols)
    transposed_conv(at, w, stack, piece_refs(pieces), cols, full)


def filter_products(at, stack, full, rows, keep, send):
    for slot, out in enumerate((keep, send)):
        half = lax.rem(at[4] + slot, 2)
        place = pl.ds(pl.multiple_of(half * 2 * W, 2 * W), 2 * W)
        cells = jnp.concatenate([full[r, place, :] for r in rows], axis=1)
        part = lax.dot_general(
            stack[...], cells, (((1,), (1,)), ((), ())), preferred_element_type=F32
        ).astype(BF)
        out[:STACK, :] = part[:, :W]
        out[STACK:, :] = part[:, W:]


def filter_kernel(at, stack, full, keep, send):
    filter_products(at, stack, full, range(1, ROWS + 1), keep, send)


def gathered_filter_kernel(at, stack, *refs):
    pieces, (keep, send, full) = refs[:4], refs[4:]
    for k, piece in zip((0, 1, 3, 2), pieces):
        for n in range(2):
            place = pl.multiple_of(source_of(at, (n, k)) * OWN, OWN)
            full[:, pl.ds(place, OWN), :] = piece[n]
    filter_products(at, stack, full, range(ROWS), keep, send)


def core_sum_kernel(at, k1, r1, k2, r2, *outs):
    for n, (k, r) in enumerate(((k1, r1), (k2, r2))):
        for dz, out in enumerate(outs):
            p = lax.rem(at[2] + dz, 4)
            rows = pl.ds(pl.multiple_of(p * PIECE, PIECE), PIECE)
            out[n] = (k[rows, :].astype(F32) + r[rows, :].astype(F32)).astype(BF)


def two_sum_kernel(a, b, out):
    out[...] = (a[...].astype(F32) + b[...].astype(F32)).astype(BF)


def four_sum_kernel(a, b, c, d, out):
    total = a[...].astype(F32) + b[...].astype(F32) + c[...].astype(F32) + d[...].astype(F32)
    out[...] = total.astype(BF)


def sum_four(a, b, c, d, name):
    return call(four_sum_kernel, dict(shapes=[(a.shape, BF)]), a, b, c, d, name=name)[0]


Z_ORDER = (0, 1, 3, 2)


def place_kernel(half, at, *refs):
    pieces, (first, second, wide, sems) = refs[:4], refs[-4:]
    core = lax.rem(at[4] + half, 2)
    copies = []
    for k, dz in enumerate(Z_ORDER):
        z = lax.rem(at[2] + 4 - dz, 4)
        rows = pl.ds(pl.multiple_of(lax.rem(z, 2) * PIECE, PIECE), PIECE)
        lanes = pl.ds(pl.multiple_of((core * 2 + lax.div(z, 2)) * W, W), W)
        for n, out in enumerate((first, second)):
            wide[k, n] = pieces[k][n].astype(F32)
            copies.append(
                pltpu.make_async_copy(wide.at[k, n], out.at[rows, lanes], sems.at[k, n])
            )
            copies[-1].start()
    for copy in copies:
        copy.wait()


def place(half, at, pieces, outs, name):
    whole = jax.ShapeDtypeStruct((STACK, C), F32)
    anywhere = pl.BlockSpec(memory_space=pl.ANY)
    return pl.pallas_call(
        functools.partial(place_kernel, half),
        out_shape=[whole] * 2,
        in_specs=[SMEM] + [VMEM] * 4 + [anywhere] * len(outs),
        out_specs=[anywhere] * 2,
        input_output_aliases={5 + n: n for n in range(len(outs))},
        scratch_shapes=[pltpu.VMEM((4, 2, PIECE, W), F32), pltpu.SemaphoreType.DMA((4, 2))],
        compiler_params=pltpu.CompilerParams(vmem_limit_bytes=10 * 1024 * 1024),
        cost_estimate=hint(name),
        name=name,
    )(at, *pieces, *outs)


def gather_ch(value):
    other = lax.ppermute(value, "ch", ch_pairs(1, 0))
    near = [lax.ppermute(value, "ch", ch_pairs(0, k)) for k in (1, 3, 2)]
    far = [lax.ppermute(other, "ch", ch_pairs(0, k)) for k in (1, 3, 2)]
    return [value, other, *near, *far]


def gather_ch_pairs(value):
    both = jnp.stack([value, lax.ppermute(value, "ch", ch_pairs(1, 0))])
    return [both] + [lax.ppermute(both, "ch", ch_pairs(0, k)) for k in (1, 3, 2)]


def scatter_sum_kernel(own, a, b, c, near, far):
    for n, out in enumerate((near, far)):
        total = own[n].astype(F32) + a[n].astype(F32) + b[n].astype(F32) + c[n].astype(F32)
        out[...] = total.astype(out.dtype)


def scatter_ch(pieces, name, gate=None):
    got = [lax.ppermute(p, "ch", ch_pairs(0, k)) for k, p in zip((1, 3, 2), pieces[1:])]
    own = pieces[0] if gate is None else after(pieces[0], gate)
    near, far = call(
        scatter_sum_kernel, dict(shapes=[((ROWS, OWN, W), F32), ((ROWS, OWN, W), BF)]),
        own, *got, name=name,
    )
    return near, lax.ppermute(far, "ch", ch_pairs(1, 0)), got


def neighbours(first, last):
    up = [(i, i + 1) for i in range(15)]
    down = [(i + 1, i) for i in range(15)]
    return lax.ppermute(last, "rows", up), lax.ppermute(first, "rows", down)


def sum_rows_near(value):
    for dz, dx, dc in ((0, 0, 1), (0, 1, 0)):
        value = value + lax.ppermute(value, "rows", row_pairs(dz, dx, dc))
    return value


def sum_rows_far(value, gate=None):
    for mask in (4, 8):
        if mask == 8 and gate is not None:
            value = after(value, gate)
        value = value + lax.ppermute(value, "rows", [(i, i ^ mask) for i in range(16)])
    return value


def final_kernel(near, far, out):
    out[...] = jnp.swapaxes(near[...] + far[...].astype(F32), 0, 1).astype(BF)


def input_grad(kernel, w, *args, name):
    outs = call(
        kernel,
        dict(
            shapes=[((STACK, ROWS * W), BF)] + [((2, ROWS, OWN, W), BF)] * 4,
            scratch=[pltpu.VMEM((3, ROWS + 2, OWN, W), BF), pltpu.VMEM((ROWS, C, W), BF)],
        ),
        *args, w,
        name=name,
    )
    return outs[0], outs[1:]


def body(x_band, first_filter, second_filter, norm_gain, norm_shift, out_cotangent):
    cells = float((C // G) * ROWS * lax.axis_size("rows") * W)
    ch, rows = lax.axis_index("ch"), lax.axis_index("rows")
    at = jnp.stack([ch // 4, ch % 4, rows // 4, (rows // 2) % 2, rows % 2, rows]).astype(jnp.int32)
    x_band, out_cotangent, at = lax.optimization_barrier((x_band, out_cotangent, at))
    x_above, x_below = neighbours(
        *(jnp.concatenate([x_band[:, r], out_cotangent[:, r]]) for r in (0, ROWS - 1))
    )
    cot_rows = jnp.transpose(out_cotangent, (1, 0, 2))
    x_rows = jnp.concatenate(
        [x_above[None, :OWN], jnp.transpose(x_band, (1, 0, 2)), x_below[None, :OWN]]
    )
    w1 = first_filter.reshape(STACK, C)
    w2 = second_filter.reshape(STACK, C)
    gain = jnp.broadcast_to(norm_gain[:, None], (OWN, W))
    shift = jnp.broadcast_to(norm_shift[:, None], (OWN, W))
    strip = (ROWS, OWN, W)

    x_pieces = gather_ch(x_rows)
    cot_stack, act_pieces = input_grad(
        act_grad_kernel, w2, at, after(cot_rows, x_pieces[4]), x_above, x_below, name="act_grad"
    )
    hid, stats, x_full = call(
        conv_kernel,
        dict(
            shapes=[(strip, F32), ((8, W), F32), ((ROWS + 2, C, W), BF)],
            scratch=[pltpu.VMEM((3, ROWS, OWN, W), F32)],
        ),
        at, *x_pieces, w1,
        name="hidden",
    )
    stats = sum_rows_near(stats)
    *act_parts, _ = scatter_ch(act_pieces, "act_grad_sum", stats)
    stats = sum_rows_far(stats, act_parts[0])
    (act,) = call(
        functools.partial(act_kernel, cells), dict(shapes=[(strip, BF)]),
        hid, stats, gain, shift, name="activation",
    )
    pre, sums = call(
        functools.partial(pre_kernel, cells), dict(shapes=[(strip, F32), ((8, W), F32)]),
        hid, stats, gain, shift, *act_parts, name="pre_grad",
    )
    act_all = gather_ch_pairs(act)
    sums = sum_rows_near(sums)
    sums = after(sums, act_all[0])
    sums = sum_rows_far(sums)
    above, below = neighbours(
        jnp.stack([pre[0], hid[0]]), jnp.stack([pre[ROWS - 1], hid[ROWS - 1]])
    )
    half = ((2 * STACK, W), BF)
    hg_stack, band_pieces = input_grad(
        functools.partial(band_grad_kernel, cells), w1,
        at, hid, stats, gain, pre, after(sums, act_all[1:3]), above, below,
        name="band_grad",
    )
    keep1, send1 = call(
        filter_kernel, dict(shapes=[half, half]), at, hg_stack, x_full,
        name="first_grad",
    )
    recv1 = lax.ppermute(send1, "rows", row_pairs(0, 0, 1))
    keep2, send2 = call(
        gathered_filter_kernel,
        dict(shapes=[half, half], scratch=[pltpu.VMEM((ROWS, C, W), BF)]),
        at, cot_stack, *act_all,
        name="second_grad",
    )
    recv2 = lax.ppermute(send2, "rows", row_pairs(0, 0, 1))
    share = ((2, PIECE, W), BF)
    parts = call(
        core_sum_kernel, dict(shapes=[share] * 4), at, keep1, recv1, keep2, recv2, name="core_sum"
    )
    got = [lax.ppermute(parts[k], "rows", row_pairs(k, 0, 0)) for k in (1, 3, 2)]
    *band_parts, band_got = scatter_ch([after(p, parts[0]) for p in band_pieces], "band_grad_sum")
    gain_grad, shift_grad = sums[0, :OWN], sums[0, OWN:]
    part = sum_four(after(parts[0], (gain_grad, shift_grad)), *got, name="filter_sum")
    part = call(
        two_sum_kernel, dict(shapes=[share]),
        part, lax.ppermute(part, "rows", row_pairs(0, 1, 0)), name="pair_sum",
    )[0]
    mine = [part] + [lax.ppermute(part, "rows", row_pairs(k, 0, 0)) for k in Z_ORDER[1:]]
    theirs = [lax.ppermute(p, "rows", row_pairs(0, 0, 1)) for p in mine]
    grads = place(0, at, mine, (), "own_half")
    first_grad, second_grad = place(1, at, theirs, grads, "other_half")
    (band,) = call(final_kernel, dict(shapes=[((OWN, ROWS, W), BF)]), *band_parts, name="band_grad_total")
    shape = (3, 3, OWN, C)
    return (
        band,
        first_grad.reshape(shape),
        second_grad.reshape(shape),
        gain_grad,
        shift_grad,
    )


def solution(mesh):
    filters = P(None, None, "ch", None)
    strip = P("ch", "rows", None)
    return jax.shard_map(
        body,
        mesh=mesh,
        in_specs=(strip, filters, filters, P("ch"), P("ch"), strip),
        out_specs=(strip, filters, filters, P("ch"), P("ch")),
        check_vma=False,
    )
```
